256 devices in a mesh: replica: 32 (over z, x), fsdp: 8 (over y, core).
Axes of the slice: x: 4, y: 4, z: 8, core: 2. Of those that a mesh axis runs over, the one named last changes fastest.
Arguments:
- features: bfloat16 [65536, 2560], P(('replica', 'fsdp')), may hold values from -0.125 to 0.125
- cotangent: bfloat16 [65536, 2560], P(('replica', 'fsdp')), may hold values from -6 to 6
- weight: bfloat16 [2560, 2560], P('fsdp'), may hold values from -0.125 to 0.125
- feedback: float32 [81920, 2560], P(('replica', 'fsdp')), may hold values from -6 to 6
- start_factors: float32 [2560, 32], replicated, may hold values from -6 to 6
Outputs:
- input_grad: bfloat16 [65536, 2560], P(('replica', 'fsdp'))
- new_feedback: float32 [81920, 2560], P(('replica', 'fsdp'))
- q_factor: float32 [2560, 32], replicated
The draws below stay inside these ranges and needn't reach their ends.
All inputs are finite; a program needn't handle non-finite values.
Results may differ from the reference program's by a relative error of at most 0.0005.
Values may be sent and summed in bfloat16 or wider, within the bound.
No kernel may reach another device: no remote copies, remote signals or barrier semaphores. Data moves between devices by JAX's collectives and lax.ppermute only.
A program may use at most 128 MiB of HBM per device.

```python
import jax
import jax.numpy as jnp
from jax import lax

DIN = 2560
DOUT = 2560
RANK = 32
TOK_DEV = 256
TOKENS = 65536
N_REPLICA = 32
N_FSDP = 8


def steps_of(own_key, extent, cuts, smallest, high):
    gain, own = 1.0, jax.random.fold_in(own_key, 6)
    for dim, parts in cuts:
        steps = jnp.exp(jax.random.uniform(jax.random.fold_in(own, dim), (parts,), jnp.float32, smallest / len(cuts), high / len(cuts)))
        gain = gain * jnp.repeat(steps, extent[dim] // parts).reshape([-1 if axis == dim else 1 for axis in range(len(extent))])
    return gain


def normal_values(key, shape, width, most, cuts=(), kind=jnp.bfloat16):
    array = width * jax.random.normal(key, shape, jnp.float32)
    if cuts:
        array = array * steps_of(key, shape, cuts, -0.22, 0.18)
    return jnp.clip(array, -most, most).astype(kind)


def setup_inputs(seed: int = 0) -> dict:
    key_list = jax.random.split(jax.random.key(seed), 6)
    features = normal_values(key_list[0], (TOKENS, DIN), ((TOK_DEV * N_FSDP) ** -0.5), 0.125, ((0, 256),))
    cotangent = normal_values(key_list[1], (TOKENS, DOUT), 1.0, 6.0, ((0, 256),))
    weight = normal_values(key_list[2], (DIN, DOUT), DOUT ** -0.5, 0.125, ((0, 8),))
    feedback = normal_values(key_list[3], (N_REPLICA * DIN, DOUT), 1.0, 6.0, ((0, 256),), jnp.float32)
    start_factors = normal_values(key_list[4], (DOUT, RANK), 1.0, 6.0, (), jnp.float32)
    return dict(features=features, cotangent=cotangent, weight=weight, feedback=feedback, start_factors=start_factors)


def reference(features, cotangent, weight, feedback, start_factors):
    highest = lax.Precision.HIGHEST
    input_grad = jnp.dot(cotangent.astype(jnp.float32), weight.T.astype(jnp.float32), preferred_element_type=jnp.float32).astype(jnp.bfloat16)
    blocks_x = features.reshape(N_REPLICA, N_FSDP, TOK_DEV, DIN)
    blocks_g = cotangent.reshape(N_REPLICA, N_FSDP, TOK_DEV, DOUT)
    errors = feedback.reshape(N_REPLICA, DIN, DOUT)

    def build(item):
        rep_x, rep_g, rep_e = item

        def accumulate(total, pair):
            block_x, block_g = pair
            partial_value = jnp.dot(block_x.T.astype(jnp.float32), block_g.astype(jnp.float32), preferred_element_type=jnp.float32)
            return (total + partial_value, None)
        total, unused = lax.scan(accumulate, jnp.zeros((DIN, DOUT), jnp.float32), (rep_x, rep_g))
        return total + rep_e
    grown = lax.map(build, (blocks_x, blocks_g, errors))
    psum = jnp.einsum('rij,jk->ik', grown, start_factors, precision=highest)
    gram = jnp.dot(psum.T, psum, precision=highest)
    lower = jnp.linalg.cholesky(gram)
    ortho = lax.linalg.triangular_solve(lower, psum, left_side=False, lower=True, transpose_a=True)
    q_factor = jnp.einsum('rij,ik->jk', grown, ortho, precision=highest) / N_REPLICA
    approx = jnp.dot(ortho, q_factor.T, precision=highest)
    new_feedback = (grown - approx[None]).reshape(N_REPLICA * DIN, DOUT)
    return (input_grad, new_feedback, q_factor)
```

```python
import jax
import jax.numpy as jnp
from jax import lax
from jax.sharding import Mesh, PartitionSpec as P

HIGHEST = lax.Precision.HIGHEST
FSDP = ("y", "core")
ALL = ("z", "x", "y", "core")


def dot(a, b, ca, cb, precision=HIGHEST):
    return lax.dot_general(
        a, b, (((ca,), (cb,)), ((), ())), precision=precision, preferred_element_type=jnp.float32
    )


def exchange(u, axes):
    return lax.all_to_all(u, axes, 0, 0, tiled=True)


def swap_cores(v):
    return lax.ppermute(v, "core", [(0, 1), (1, 0)])


def sum_all(v):
    core = lax.axis_index("core")
    tiles = v.reshape(4, 8, 20, 128).transpose(0, 2, 1, 3).reshape(2, 16, 20, 128)
    mine = lax.dynamic_index_in_dim(tiles, core, 0, False)
    other = lax.dynamic_index_in_dim(tiles, 1 - core, 0, False)
    half = mine + swap_cores(other)
    part = exchange(half, ("x", "y")).sum(0)
    part = exchange(jnp.broadcast_to(part[None], (8, 20, 128)), "z").sum(0)
    half = exchange(jnp.broadcast_to(part[None], (16, 20, 128)), ("x", "y"))
    other = swap_cores(half)
    whole = jnp.where(core == 0, jnp.stack([half, other]), jnp.stack([other, half]))
    return whole.reshape(4, 20, 8, 128).transpose(0, 2, 1, 3).reshape(32, 2560)


def shards(features, cotangent, weight, feedback, start_factors):
    f32 = jnp.float32
    place = lax.axis_index(FSDP) * 320
    gathered = lax.all_gather(cotangent, FSDP, axis=0, tiled=True)
    columns = exchange(features.reshape(256, 8, 320).transpose(1, 0, 2), FSDP).reshape(2048, 320)

    x32, c32 = features.astype(f32), cotangent.astype(f32)
    small = dot(c32, start_factors, 1, 0)
    local = dot(small, x32, 0, 0)
    own = dot(start_factors, feedback, 0, 1)
    local = local + lax.dynamic_update_slice(jnp.zeros_like(local), own, (0, place))
    psum = sum_all(local)

    psum_own = lax.dynamic_slice(psum, (0, place), (32, 320))
    small = dot(psum, x32, 1, 1)
    local = dot(small, c32, 1, 0) + dot(psum_own, feedback, 1, 0)
    right = sum_all(local)

    gram = dot(psum, psum, 1, 1)
    lower = jnp.linalg.cholesky(gram)
    inverse = lax.linalg.triangular_solve(lower, jnp.eye(32, dtype=f32), left_side=True, lower=True)
    ortho = dot(inverse, psum_own, 1, 0)
    q_factor = dot(inverse, right, 1, 0) / 32

    grown = dot(columns, gathered, 0, 0, None) + feedback
    new_feedback = grown - dot(ortho, q_factor, 0, 0)

    back = dot(gathered, weight, 1, 1, None).astype(jnp.bfloat16)
    input_grad = exchange(back.reshape(8, 256, 320), FSDP).transpose(1, 0, 2).reshape(256, 2560)
    return (input_grad, new_feedback, q_factor.T)


def solution(mesh):
    split = Mesh(mesh.devices.reshape(8, 4, 4, 2), ALL)
    placed = (P(ALL, None), P(ALL, None), P(FSDP, None), P(ALL, None), P())
    return jax.shard_map(
        shards,
        mesh=split,
        in_specs=placed,
        out_specs=(P(ALL, None), P(ALL, None), P()),
        check_vma=False,
    )
```

```python
import functools

import jax
import jax.numpy as jnp
from jax import lax
from jax.experimental import pallas as pl
from jax.experimental.pallas import tpu as pltpu
from jax.sharding import Mesh, PartitionSpec as P

FSDP = ("y", "core")
ALL = ("z", "x", "y", "core")
BF16 = jnp.bfloat16
F32 = jnp.float32
VMEM = pl.BlockSpec(memory_space=pltpu.VMEM)
ANY = pl.BlockSpec(memory_space=pl.ANY)
SMEM = pl.BlockSpec(memory_space=pltpu.SMEM)
AHEAD = [(2 * y + c, 2 * ((y + 1 - 2 * c) % 4) + c) for y in range(4) for c in range(2)]
BACK = [(b, a) for a, b in AHEAD]
ACROSS = [(2 * y + c, 2 * ((y + 2) % 4) + c) for y in range(4) for c in range(2)]
HALF = (16, 3, 8, 128)


def mm(a, b, ca, cb):
    return lax.dot_general(a, b, (((ca,), (cb,)), ((), ())), preferred_element_type=F32)


def terms(v):
    a = v.astype(BF16)
    rest = v - a.astype(F32)
    b = rest.astype(BF16)
    return a, b, (rest - b.astype(F32)).astype(BF16)


def stacked(v):
    return jnp.concatenate(terms(v), axis=0)


def folded(v):
    return v[0:32] + v[32:64] + v[64:96]


def put_window(place, feedback_ref, window_ref):
    core = place[0]
    zero = jnp.zeros((64, 2560), BF16)
    free = pl.multiple_of(320 * (1 - core), 64)
    first = pl.multiple_of(64 * core, 64)
    for i in range(5):
        rows = pl.ds(64 * i, 64)
        for t, term in enumerate(terms(feedback_ref[rows, :])):
            window_ref[t, pl.ds(pl.multiple_of(first + 64 * i, 64), 64), :] = term
    for t in range(3):
        window_ref[t, pl.ds(free, 64), :] = zero


def emit(core, value, mine_ref, other_ref):
    for tile in range(48):
        if tile < 40:
            r, j = divmod(tile, 20)
            low = value[8 * r : 8 * r + 8, 128 * j : 128 * j + 128]
            high = value[16 + 8 * r : 24 + 8 * r, 128 * j : 128 * j + 128]
            mine, other = jnp.where(core == 0, low, high), jnp.where(core == 0, high, low)
        else:
            mine = other = jnp.zeros((8, 128), F32)
        mine_ref[tile // 3, tile % 3] = mine
        other_ref[tile // 3, tile % 3] = other


def collect(core, mine_ref, other_ref, whole_ref):
    for tile in range(40):
        r, j = divmod(tile, 20)
        mine, other = mine_ref[tile // 3, tile % 3], other_ref[tile // 3, tile % 3]
        lanes = pl.ds(128 * j, 128)
        whole_ref[pl.ds(8 * r, 8), lanes] = jnp.where(core == 0, mine, other)
        whole_ref[pl.ds(16 + 8 * r, 8), lanes] = jnp.where(core == 0, other, mine)


def left_kernel(
    place, x_any, c_ref, s_ref, f_any, mine_ref, other_ref, window_ref, sum_ref, x_ref, f_ref, sems
):
    core, lane = place[0], pl.multiple_of(place[1], 128)
    x_copy = pltpu.make_async_copy(x_any, x_ref, sems.at[0])
    f_copy = pltpu.make_async_copy(f_any, f_ref, sems.at[1])
    x_copy.start()
    f_copy.start()
    s3 = stacked(s_ref[...])
    small = folded(mm(s3, c_ref[...], 1, 1))
    x_copy.wait()
    sum_ref[...] = folded(mm(stacked(small), x_ref[...], 1, 0))
    f_copy.wait()
    put_window(place, f_ref, window_ref)
    own = sum(folded(mm(s3, window_ref[t], 1, 1)) for t in range(3))
    sum_ref[:, pl.ds(lane, 384)] += own
    emit(core, sum_ref[...], mine_ref, other_ref)


def right_kernel(
    place, mine_ref, other_ref, x_ref, c_ref, f_ref, out_ref, away_ref, gram_ref, own_ref,
    window_ref, left_ref,
):
    core, lane = place[0], pl.multiple_of(place[1], 128)
    collect(core, mine_ref, other_ref, left_ref)
    left = left_ref[...]
    p3 = stacked(left)
    small = folded(mm(p3, x_ref[...], 1, 1))
    total = folded(mm(stacked(small), c_ref[...], 1, 0))
    put_window(place, f_ref, window_ref)
    own = left_ref[:, pl.ds(lane, 384)]
    own_ref[...] = own
    own3 = stacked(own)
    total += sum(folded(mm(own3, window_ref[t], 1, 0)) for t in range(3))
    emit(core, total, out_ref, away_ref)
    gram_ref[...] = sum(folded(mm(p3, p3[32 * t : 32 * t + 32], 1, 1)) for t in range(3))


def rows_kernel(
    place, x0, x1, x2, x3, c0, c1, c2, c3, f_ref, mine_ref, other_ref, turned, joined, full
):
    core = place[0]

    @pl.when(pl.program_id(0) == 0)
    def _():
        for k, x in enumerate((x0, x1, x2, x3)):
            turned[:, pl.ds(256 * k, 256)] = x[...].T

    for k, c in enumerate((c0, c1, c2, c3)):
        joined[pl.ds(256 * k, 256), :] = c[...]
    full[...] = mm(turned[...], joined[...], 1, 0)
    mine_ref[...] = full[pl.ds(pl.multiple_of(320 * core, 64), 320), :] + f_ref[...]
    other_ref[...] = full[pl.ds(pl.multiple_of(320 * (1 - core), 64), 320), :]


def back_kernel(n, place, *refs):
    cs, (w_ref, swapped_ref), outs, (both, totals) = refs[:n], refs[n : n + 2], refs[n + 2 : -2], refs[-2:]
    core, k = place[0], pl.program_id(0)
    both[pl.ds(pl.multiple_of(320 * core, 64), 320), :] = w_ref[...]
    both[pl.ds(pl.multiple_of(320 * (1 - core), 64), 320), :] = swapped_ref[...]
    for i in range(n):
        part = mm(cs[i][...], both[...], 1, 1)

        @pl.when(k == 0)
        def _():
            totals[i] = part

        @pl.when((k > 0) & (k < 4))
        def _():
            totals[i] += part

        @pl.when(k == 4)
        def _():
            outs[i][...] = (totals[i] + part).astype(BF16)


def back_columns(place, cs, weight, swapped):
    n = len(cs)
    block = pl.BlockSpec((256, 512), lambda i: (0, i))
    rows = pl.BlockSpec((320, 512), lambda i: (0, i))
    return pl.pallas_call(
        functools.partial(back_kernel, n),
        grid=(5,),
        in_specs=[SMEM] + [block] * n + [rows] * 2,
        out_specs=[pl.BlockSpec((256, 640), lambda i: (0, 0))] * n,
        out_shape=[jax.ShapeDtypeStruct((256, 640), BF16)] * n,
        scratch_shapes=[pltpu.VMEM((640, 512), BF16), pltpu.VMEM((n, 256, 640), F32)],
        compiler_params=pltpu.CompilerParams(vmem_limit_bytes=60 << 20),
        cost_estimate=pl.CostEstimate(flops=n * 84 * 10**7, bytes_accessed=(4 + n) << 20, transcendentals=0),
    )(place, *cs, weight, swapped)


def place_kernel(chips, g0, g1, g2, g3, out_ref):
    for k, g in enumerate((g0, g1, g2, g3)):
        out_ref[:, pl.ds(pl.multiple_of(640 * chips[k], 128), 640)] = g[...]


def placed_columns(chips, blocks):
    return pl.pallas_call(
        place_kernel,
        in_specs=[SMEM] + [VMEM] * 4,
        out_specs=VMEM,
        out_shape=jax.ShapeDtypeStruct((256, 2560), BF16),
        cost_estimate=pl.CostEstimate(flops=0, bytes_accessed=3 << 20, transcendentals=0),
    )(chips, *blocks)


def last_kernel(
    place, mine_ref, other_ref, inverse_ref, ortho_ref, a_ref, b_ref, new_ref, q_ref,
    right_ref, lhs_ref, rhs_ref,
):
    @pl.when(pl.program_id(0) == 0)
    def _():
        collect(place[0], mine_ref, other_ref, right_ref)
        i1, i2, i3 = terms(inverse_ref[...])
        r1, r2, r3 = terms(right_ref[...])
        q = sum(mm(a, b, 1, 0) for a, b in ((i1, r1), (i1, r2), (i2, r1), (i2, r2), (i1, r3), (i3, r1)))
        q = q / 32
        q_ref[...] = q
        q1, q2, q3 = terms(q)
        o1, o2, o3 = terms(ortho_ref[...])
        for k, (o, q) in enumerate(((o1, q1), (o1, q2), (o2, q1), (o2, q2), (o1, q3), (o3, q1))):
            lhs_ref[:, pl.ds(32 * k, 32)] = o
            rhs_ref[pl.ds(32 * k, 32), :] = q

    rows = pl.ds(pl.multiple_of(64 * pl.program_id(0), 64), 64)
    new_ref[...] = a_ref[...] + b_ref[...] - mm(lhs_ref[rows, :], rhs_ref[...], 1, 0)


def call(kernel, ins, outs, scratch, flops, size):
    return pl.pallas_call(
        kernel,
        in_specs=[SMEM] + ins,
        out_specs=[VMEM] * len(outs),
        out_shape=[jax.ShapeDtypeStruct(s, F32) for s in outs],
        scratch_shapes=scratch,
        compiler_params=pltpu.CompilerParams(vmem_limit_bytes=40 << 20),
        cost_estimate=pl.CostEstimate(flops=flops, bytes_accessed=size, transcendentals=0),
    )


def left_product(place, x, c, s, f):
    return call(
        left_kernel, [ANY, VMEM, VMEM, ANY], [HALF, HALF],
        [pltpu.VMEM((3, 384, 2560), BF16), pltpu.VMEM((32, 2560), F32),
         pltpu.VMEM((256, 2560), BF16), pltpu.VMEM((320, 2560), F32), pltpu.SemaphoreType.DMA((2,))],
        2 * 10**9, 7 << 20,
    )(place, x, c, s, f)


def right_product(place, mine, other, x, c, f):
    return call(
        right_kernel, [VMEM] * 5, [HALF, HALF, (32, 32), (32, 384)],
        [pltpu.VMEM((3, 384, 2560), BF16), pltpu.VMEM((32, 2560), F32)], 2 * 10**9, 7 << 20,
    )(place, mine, other, x, c, f)


def gradient_rows(place, xs, cs, feedback):
    whole = pl.BlockSpec((256, 640), lambda i: (0, 0))
    part = pl.BlockSpec((256, 256), lambda i: (0, i))
    rows = pl.BlockSpec((320, 256), lambda i: (0, i))
    return pl.pallas_call(
        rows_kernel,
        grid=(10,),
        in_specs=[SMEM] + [whole] * 4 + [part] * 4 + [rows],
        out_specs=[rows, rows],
        out_shape=[jax.ShapeDtypeStruct((320, 2560), F32)] * 2,
        scratch_shapes=[pltpu.VMEM((640, 1024), BF16), pltpu.VMEM((1024, 256), BF16),
                        pltpu.VMEM((640, 256), F32)],
        compiler_params=pltpu.CompilerParams(vmem_limit_bytes=60 << 20),
        cost_estimate=pl.CostEstimate(flops=34 * 10**8, bytes_accessed=17 << 20, transcendentals=0),
    )(place, *xs, *cs, feedback)


def last_step(place, mine, other, inverse, ortho, a, b):
    part = pl.BlockSpec((64, 2560), lambda i: (i, 0))
    half = pl.BlockSpec(HALF, lambda i: (0, 0, 0, 0))
    return pl.pallas_call(
        last_kernel,
        grid=(5,),
        in_specs=[SMEM, half, half, pl.BlockSpec((32, 32), lambda i: (0, 0)),
                  pl.BlockSpec((320, 32), lambda i: (0, 0)), part, part],
        out_specs=[part, pl.BlockSpec((32, 2560), lambda i: (0, 0))],
        out_shape=[jax.ShapeDtypeStruct((320, 2560), F32), jax.ShapeDtypeStruct((32, 2560), F32)],
        scratch_shapes=[pltpu.VMEM((32, 2560), F32), pltpu.VMEM((320, 192), BF16),
                        pltpu.VMEM((192, 2560), BF16)],
        compiler_params=pltpu.CompilerParams(vmem_limit_bytes=32 << 20),
        cost_estimate=pl.CostEstimate(flops=3 * 10**8, bytes_accessed=10 << 20, transcendentals=0),
    )(place, mine, other, inverse, ortho, a, b)


def exchange(u, axes):
    return lax.all_to_all(u, axes, 0, 0, tiled=True)


def swap(v):
    return lax.ppermute(v, "core", [(0, 1), (1, 0)])


def send(v, pairs):
    return lax.ppermute(v, FSDP, pairs)


def tie(*values):
    return lax.optimization_barrier(values)


def second(v):
    return exchange(jnp.broadcast_to(v.sum(0)[None], (8, 3, 8, 128)), "z")


def third(v):
    return exchange(jnp.broadcast_to(v.sum(0)[None], HALF), ("x", "y"))


def shards(features, cotangent, weight, feedback, start_factors):
    core, y = lax.axis_index("core"), lax.axis_index("y")
    place = jnp.stack([core, 128 * (5 * y + 2 * core)]).astype(jnp.int32)
    ahead, back = lax.rem(y + 5 - 2 * core, 4), lax.rem(y + 3 + 2 * core, 4)
    across = lax.rem(y + 2, 4)

    def columns(chip):
        return lax.dynamic_slice(features, (0, 640 * chip), (256, 640))

    c1, c2 = send(cotangent, AHEAD), send(cotangent, BACK)
    swapped = swap(weight)

    mine, other = left_product(place, features, cotangent, start_factors.T, feedback)
    half = exchange(mine + swap(other), ("x", "y"))
    (g0,) = back_columns(place, (cotangent,), weight, swapped)
    half, g0, features_later = tie(half, g0, features)

    def columns(chip):
        return lax.dynamic_slice(features_later, (0, 640 * chip), (256, 640))

    x0 = columns(y)
    x1, x2 = send(columns(ahead), AHEAD), send(columns(back), BACK)
    x3 = send(columns(across), ACROSS)
    half = second(half)
    half, c1, c2 = tie(half, c1, c2)
    c3 = send(c1, AHEAD)
    half = third(half)
    g1, g2 = back_columns(place, (c1, c2), weight, swapped)
    half, g1, g2 = tie(half, g1, g2)
    u1, u2 = send(g1, BACK), send(g2, AHEAD)

    mine, other, gram, own = right_product(place, half, swap(half), features, cotangent, feedback)
    half = exchange(mine + swap(other), ("x", "y"))
    lower = jnp.linalg.cholesky(gram)
    inverse = lax.linalg.triangular_solve(lower, jnp.eye(32, dtype=F32), left_side=True, lower=True)
    ortho = lax.dot_general(
        own, inverse, (((0,), (1,)), ((), ())), precision=lax.Precision.HIGHEST,
        preferred_element_type=F32,
    )
    ortho = lax.dynamic_slice(ortho, (64 * core, 0), (320, 32))
    half, ortho, inverse, c3, x1, x2, x3 = tie(half, ortho, inverse, c3, x1, x2, x3)
    half = second(half)
    (g3,) = back_columns(place, (c3,), weight, swapped)
    grown, away = gradient_rows(place, (x0, x1, x2, x3), (cotangent, c1, c2, c3), feedback)
    half, grown, away, g3, u1, u2 = tie(half, grown, away, g3, u1, u2)
    away, u3 = swap(away), send(g3, ACROSS)
    half = third(half)
    half, away, u3 = tie(half, away, u3)

    new_feedback, q_factor = last_step(place, half, swap(half), inverse, ortho, grown, away)
    chips = jnp.stack([y, ahead, back, across]).astype(jnp.int32)
    input_grad = placed_columns(chips, (g0, u1, u2, u3))
    return (input_grad, new_feedback, q_factor.T)


def solution(mesh):
    split = Mesh(mesh.devices.reshape(8, 4, 4, 2), ALL)
    placed = (P(ALL, None), P(ALL, None), P(FSDP, None), P(ALL, None), P())
    return jax.shard_map(
        shards,
        mesh=split,
        in_specs=placed,
        out_specs=(P(ALL, None), P(ALL, None), P()),
        check_vma=False,
    )
```

```python
import functools

import jax
import jax.numpy as jnp
from jax import lax
from jax.experimental import pallas as pl
from jax.experimental.pallas import tpu as pltpu
from jax.sharding import Mesh, PartitionSpec as P

FSDP = ("y", "core")
ALL = ("z", "x", "y", "core")
BF16 = jnp.bfloat16
F32 = jnp.float32
VMEM = pl.BlockSpec(memory_space=pltpu.VMEM)
ANY = pl.BlockSpec(memory_space=pl.ANY)
SMEM = pl.BlockSpec(memory_space=pltpu.SMEM)
AHEAD = [(2 * y + c, 2 * ((y + 1 - 2 * c) % 4) + c) for y in range(4) for c in range(2)]
BACK = [(b, a) for a, b in AHEAD]
ACROSS = [(2 * y + c, 2 * ((y + 2) % 4) + c) for y in range(4) for c in range(2)]
HALF = (16, 3, 8, 128)


def mm(a, b, ca, cb):
    return lax.dot_general(a, b, (((ca,), (cb,)), ((), ())), preferred_element_type=F32)


def terms(v):
    a = v.astype(BF16)
    rest = v - a.astype(F32)
    b = rest.astype(BF16)
    return a, b, (rest - b.astype(F32)).astype(BF16)


def stacked(v):
    return jnp.concatenate(terms(v), axis=0)


def folded(v):
    return v[0:32] + v[32:64] + v[64:96]


def two_terms(v):
    return jnp.concatenate(terms(v)[:2], axis=0)


def put_window(place, feedback_ref, window_ref):
    core = place[0]
    zero = jnp.zeros((64, 2560), BF16)
    free = pl.multiple_of(320 * (1 - core), 64)
    first = pl.multiple_of(64 * core, 64)
    for i in range(5):
        rows = pl.ds(64 * i, 64)
        for t, term in enumerate(terms(feedback_ref[rows, :])[:2]):
            window_ref[t, pl.ds(pl.multiple_of(first + 64 * i, 64), 64), :] = term
    for t in range(2):
        window_ref[t, pl.ds(free, 64), :] = zero


class Copies:
    def __init__(self, sems):
        self.sems, self.made = sems, []

    def start(self, source, target):
        copy = pltpu.make_async_copy(source, target, self.sems.at[len(self.made)])
        copy.start()
        self.made.append(copy)
        return copy


def wait(copies):
    for copy in copies:
        copy.wait()


def emit(core, value, mine_ref, other_ref):
    for tile in range(48):
        if tile < 40:
            r, j = divmod(tile, 20)
            low = value[8 * r : 8 * r + 8, 128 * j : 128 * j + 128]
            high = value[16 + 8 * r : 24 + 8 * r, 128 * j : 128 * j + 128]
            mine, other = jnp.where(core == 0, low, high), jnp.where(core == 0, high, low)
        else:
            mine = other = jnp.zeros((8, 128), F32)
        mine_ref[tile // 3, tile % 3] = mine
        other_ref[tile // 3, tile % 3] = other


def collect(core, mine_ref, other_ref, whole_ref):
    for tile in range(40):
        r, j = divmod(tile, 20)
        mine, other = mine_ref[tile // 3, tile % 3], other_ref[tile // 3, tile % 3]
        lanes = pl.ds(128 * j, 128)
        whole_ref[pl.ds(8 * r, 8), lanes] = jnp.where(core == 0, mine, other)
        whole_ref[pl.ds(16 + 8 * r, 8), lanes] = jnp.where(core == 0, other, mine)


def left_kernel(
    place, x_any, c_any, s_ref, f_any, mine_ref, other_ref, sum_ref, x_ref, f_ref, c_ref, sems
):
    core, lane = place[0], pl.multiple_of(place[1], 128)
    copies = Copies(sems)

    def fetch(source, target, parts, rows):
        return [copies.start(source.at[pl.ds(rows * k, rows)], target.at[pl.ds(rows * k, rows)]) for k in parts]

    c_in = fetch(c_any, c_ref, range(4), 64)
    f_in = fetch(f_any, f_ref, range(10), 32)
    x_in = fetch(x_any, x_ref, range(4), 64)
    factors = jnp.concatenate(terms(s_ref[...].T), axis=1)
    wait(c_in)
    small = folded(mm(c_ref[...], factors, 1, 0).T)
    parts = []
    for k in range(2):
        wait(f_in[5 * k : 5 * k + 5])
        part = mm(two_terms(f_ref[pl.ds(160 * k, 160), :]), factors, 1, 0)
        parts.append(part[:160] + part[160:])
    own = folded(jnp.concatenate(parts, axis=0).T)
    zero = jnp.zeros((32, 64), F32)
    own = jnp.where(
        core == 0, jnp.concatenate([own, zero], axis=1), jnp.concatenate([zero, own], axis=1)
    )
    wait(x_in)
    sum_ref[...] = folded(mm(stacked(small), x_ref[...], 1, 0))
    sum_ref[:, pl.ds(lane, 384)] += own
    emit(core, sum_ref[...], mine_ref, other_ref)


def right_kernel(
    place, mine_ref, other_ref, x_ref, c_ref, f_any, out_ref, away_ref, gram_ref, own_ref,
    window_ref, left_ref, f_ref, sem,
):
    core, lane = place[0], pl.multiple_of(place[1], 128)
    f_in = pltpu.make_async_copy(f_any, f_ref, sem)
    f_in.start()
    collect(core, mine_ref, other_ref, left_ref)
    left = left_ref[...]
    p3 = stacked(left)
    small = folded(mm(p3, x_ref[...], 1, 1))
    total = folded(mm(stacked(small), c_ref[...], 1, 0))
    f_in.wait()
    put_window(place, f_ref, window_ref)
    own = left_ref[:, pl.ds(lane, 384)]
    own_ref[...] = own
    own3 = stacked(own)
    total += sum(folded(mm(own3, window_ref[t], 1, 0)) for t in range(2))
    emit(core, total, out_ref, away_ref)
    gram_ref[...] = sum(folded(mm(p3, p3[32 * t : 32 * t + 32], 1, 1)) for t in range(3))


def rows_kernel(place, *refs):
    xs, cs, f_any, mine_any, away_any = refs[:4], refs[4:8], refs[8], refs[9], refs[10]
    x_ref, turned, c_ref, f_ref, out_ref, sems = refs[11:]
    core, copies = place[0], Copies(sems)
    x_in = [copies.start(x, x_ref.at[pl.ds(256 * k, 256)]) for k, x in enumerate(xs)]
    parts = []
    for j in range(4):
        lanes = pl.ds(640 * j, 640)
        parts.append([copies.start(c.at[:, lanes], c_ref.at[pl.ds(256 * k, 256), lanes]) for k, c in enumerate(cs)])
    f_in = copies.start(f_any, f_ref)
    wait(x_in)
    first, second_ = pl.multiple_of(320 * core, 64), pl.multiple_of(320 * (1 - core), 64)
    for k in range(4):
        block = x_ref[pl.ds(256 * k, 256), :].T
        turned[pl.ds(first, 320), pl.ds(256 * k, 256)] = block[:320]
        turned[pl.ds(second_, 320), pl.ds(256 * k, 256)] = block[320:]
    sent = []
    for j in range(4):
        lanes = pl.ds(640 * j, 640)
        wait(parts[j])
        out_ref[1, :, lanes] = mm(turned[pl.ds(320, 320), :], c_ref[:, lanes], 1, 0)
        sent.append(copies.start(out_ref.at[1, :, lanes], away_any.at[:, lanes]))
    f_in.wait()
    for j in range(4):
        lanes = pl.ds(640 * j, 640)
        out_ref[0, :, lanes] = mm(turned[pl.ds(0, 320), :], c_ref[:, lanes], 1, 0) + f_ref[:, lanes]
        sent.append(copies.start(out_ref.at[0, :, lanes], mine_any.at[:, lanes]))
    wait(sent)


def gradient_rows(place, xs, cs, feedback):
    return pl.pallas_call(
        rows_kernel,
        in_specs=[SMEM] + [ANY] * 9,
        out_specs=[ANY] * 2,
        out_shape=[jax.ShapeDtypeStruct((320, 2560), F32)] * 2,
        scratch_shapes=[pltpu.VMEM((1024, 640), BF16), pltpu.VMEM((640, 1024), BF16),
                        pltpu.VMEM((1024, 2560), BF16), pltpu.VMEM((320, 2560), F32),
                        pltpu.VMEM((2, 320, 2560), F32), pltpu.SemaphoreType.DMA((32,))],
        compiler_params=pltpu.CompilerParams(vmem_limit_bytes=119 << 19),
        cost_estimate=pl.CostEstimate(flops=34 * 10**8, bytes_accessed=17 << 20, transcendentals=0),
    )(place, *xs, *cs, feedback)


def place_kernel(place, g0, g1, g2, g3, out_ref):
    for k, g in enumerate((g0, g1, g2, g3)):
        out_ref[:, pl.ds(pl.multiple_of(640 * place[2 + k], 128), 640)] = g[...]


def placed_columns(place, blocks):
    return pl.pallas_call(
        place_kernel,
        in_specs=[SMEM] + [VMEM] * 4,
        out_specs=VMEM,
        out_shape=jax.ShapeDtypeStruct((256, 2560), BF16),
        cost_estimate=pl.CostEstimate(flops=0, bytes_accessed=3 << 20, transcendentals=0),
    )(place, *blocks)


def last_kernel(
    place, mine_ref, other_ref, inverse_ref, ortho_ref, grown_ref, new_any, q_ref,
    right_ref, lhs_ref, rhs_ref, new_ref, sems,
):
    copies = Copies(sems)
    collect(place[0], mine_ref, other_ref, right_ref)
    i1, i2, i3 = terms(inverse_ref[...])
    r1, r2, r3 = terms(right_ref[...])
    q = sum(mm(a, b, 1, 0) for a, b in ((i1, r1), (i1, r2), (i2, r1), (i2, r2), (i1, r3), (i3, r1)))
    q = q / 32
    q_ref[...] = q
    q1, q2, q3 = terms(q)
    o1, o2, o3 = terms(ortho_ref[...].T)
    for k, (o, q) in enumerate(((o1, q1), (o1, q2), (o2, q1), (o2, q2), (o1, q3), (o3, q1))):
        lhs_ref[:, pl.ds(32 * k, 32)] = o
        rhs_ref[pl.ds(32 * k, 32), :] = q
    for k in range(5):
        rows = pl.ds(64 * k, 64)
        lhs = lhs_ref[pl.ds(pl.multiple_of(64 * place[0] + 64 * k, 64), 64), :]
        new_ref[rows, :] = grown_ref[rows, :] - mm(lhs, rhs_ref[...], 1, 0)
        copies.start(new_ref.at[rows], new_any.at[rows])
    wait(copies.made)


def call(kernel, ins, outs, scratch, flops, size, limit=80):
    return pl.pallas_call(
        kernel,
        in_specs=[SMEM] + ins,
        out_specs=[VMEM] * len(outs),
        out_shape=[jax.ShapeDtypeStruct(s, F32) for s in outs],
        scratch_shapes=scratch,
        compiler_params=pltpu.CompilerParams(vmem_limit_bytes=limit << 19),
        cost_estimate=pl.CostEstimate(flops=flops, bytes_accessed=size, transcendentals=0),
    )


def left_product(place, x, c, s, f):
    return call(
        left_kernel, [ANY, ANY, VMEM, ANY], [HALF, HALF],
        [pltpu.VMEM((32, 2560), F32), pltpu.VMEM((256, 2560), BF16),
         pltpu.VMEM((320, 2560), F32), pltpu.VMEM((256, 2560), BF16),
         pltpu.SemaphoreType.DMA((18,))],
        2 * 10**9, 7 << 20, 119,
    )(place, x, c, s, f)


def right_product(place, mine, other, x, c, f):
    return call(
        right_kernel, [VMEM] * 4 + [ANY], [HALF, HALF, (32, 32), (32, 384)],
        [pltpu.VMEM((2, 384, 2560), BF16), pltpu.VMEM((32, 2560), F32),
         pltpu.VMEM((320, 2560), F32), pltpu.SemaphoreType.DMA],
        2 * 10**9, 7 << 20, 115,
    )(place, mine, other, x, c, f)


def factor_kernel(gram_ref, own_ref, inverse_ref, ortho_ref):
    row = lax.broadcasted_iota(jnp.int32, (32, 128), 0)
    lane = lax.broadcasted_iota(jnp.int32, (32, 128), 1)
    a = jnp.concatenate([gram_ref[...], jnp.zeros((32, 96), F32)], axis=1)
    a = jnp.where(lane == row + 32, 1.0, a)
    for j in range(32):
        pivot = a[j : j + 1, :]
        scaled = pivot / jnp.sqrt(a[j : j + 1, j : j + 1])
        column = a[:, j : j + 1] / a[j : j + 1, j : j + 1]
        a = jnp.where(row == j, scaled, jnp.where(row > j, a - column * pivot, a))
    inverse = a[:, 32:64]
    inverse_ref[...] = inverse
    i1, i2, i3 = terms(inverse)
    o1, o2, o3 = terms(own_ref[...])
    pairs = ((i1, o1), (i1, o2), (i2, o1), (i2, o2), (i1, o3), (i3, o1))
    ortho_ref[...] = sum(mm(a, b, 1, 0) for a, b in pairs)


def factor(gram, own):
    return pl.pallas_call(
        factor_kernel,
        in_specs=[VMEM] * 2,
        out_specs=[VMEM] * 2,
        out_shape=[jax.ShapeDtypeStruct((32, 32), F32), jax.ShapeDtypeStruct((32, 384), F32)],
        cost_estimate=pl.CostEstimate(flops=10**7, bytes_accessed=1 << 20, transcendentals=32),
    )(gram, own)


def last_step(place, mine, other, inverse, ortho, grown):
    return pl.pallas_call(
        last_kernel,
        in_specs=[SMEM] + [VMEM] * 5,
        out_specs=[ANY, VMEM],
        out_shape=[jax.ShapeDtypeStruct((320, 2560), F32), jax.ShapeDtypeStruct((32, 2560), F32)],
        scratch_shapes=[pltpu.VMEM((32, 2560), F32), pltpu.VMEM((384, 192), BF16),
                        pltpu.VMEM((192, 2560), BF16), pltpu.VMEM((320, 2560), F32),
                        pltpu.SemaphoreType.DMA((5,))],
        compiler_params=pltpu.CompilerParams(vmem_limit_bytes=24 << 20),
        cost_estimate=pl.CostEstimate(flops=3 * 10**8, bytes_accessed=8 << 20, transcendentals=0),
    )(place, mine, other, inverse, ortho, grown)


def exchange(u, axes):
    return lax.all_to_all(u, axes, 0, 0, tiled=True)


def swap(v):
    return lax.ppermute(v, "core", [(0, 1), (1, 0)])


def send(v, pairs):
    return lax.ppermute(v, FSDP, pairs)


def tie(*values):
    return lax.optimization_barrier(values)


def repeated(v, n):
    return jnp.broadcast_to(v.sum(0)[None], (n, 3, 8, 128))


def shards(features, cotangent, weight, feedback, start_factors):
    core, y = lax.axis_index("core"), lax.axis_index("y")
    ahead, back = lax.rem(y + 5 - 2 * core, 4), lax.rem(y + 3 + 2 * core, 4)
    across = lax.rem(y + 2, 4)
    place = jnp.stack([core, 128 * (5 * y + 2 * core), y, ahead, back, across]).astype(jnp.int32)

    def columns(chip, x):
        return lax.dynamic_slice(x, (0, 640 * chip), (256, 640))

    c1, c2 = send(cotangent, AHEAD), send(cotangent, BACK)
    swapped = swap(weight)
    mine, other = left_product(place, features, cotangent, start_factors.T, feedback)

    half, later = tie(mine + swap(other), features)
    half = exchange(half, ("x", "y"))
    x0, x1, x2, x3 = (columns(chip, later) for chip in (y, ahead, back, across))
    weights = jnp.where(
        core == 0, jnp.concatenate([weight, swapped]), jnp.concatenate([swapped, weight])
    )

    def back_columns(c):
        return mm(c, weights, 1, 1).astype(BF16)

    half, weights, x0, x1, x2, x3 = tie(half, weights, x0, x1, x2, x3)
    half, x1, x2, x3 = tie(repeated(half, 8), x1, x2, x3)
    half = exchange(half, "z")
    x1, x2, x3 = send(x1, AHEAD), send(x2, BACK), send(x3, ACROSS)
    g0 = back_columns(cotangent)
    half, g0, c1, c2 = tie(half, g0, c1, c2)
    half, c1, c2 = tie(repeated(half, 16), c1, c2)
    half = exchange(half, ("x", "y"))
    c3 = send(c1, AHEAD)
    g1, g2 = back_columns(c1), back_columns(c2)
    half, g1, g2, x1, x2, x3 = tie(half, g1, g2, x1, x2, x3)

    mine, other, gram, own = right_product(place, half, swap(half), features, cotangent, feedback)
    half, gram, own, g1, g2 = tie(mine + swap(other), gram, own, g1, g2)
    half = exchange(half, ("x", "y"))
    u1, u2 = send(g1, BACK), send(g2, AHEAD)
    inverse, ortho = factor(gram, own)
    inverse, ortho, c3 = tie(inverse, ortho, c3)
    g3 = back_columns(c3)
    half, ortho, inverse, g3 = tie(half, ortho, inverse, g3)
    half, c3, g3, x1, x2, x3 = tie(repeated(half, 8), c3, g3, x1, x2, x3)
    half = exchange(half, "z")
    u3 = send(g3, ACROSS)
    grown, away = gradient_rows(place, (x0, x1, x2, x3), (cotangent, c1, c2, c3), feedback)
    half, u1, u2, grown, away = tie(half, u1, u2, grown, away)
    half, grown, away = tie(repeated(half, 16), grown, away)
    half = exchange(half, ("x", "y"))
    grown = grown + swap(away)
    input_grad = placed_columns(place, (g0, u1, u2, u3))
    half, grown, input_grad = tie(half, grown, input_grad)

    new_feedback, q_factor = last_step(place, half, swap(half), inverse, ortho, grown)
    return (input_grad, new_feedback, q_factor.T)


def solution(mesh):
    split = Mesh(mesh.devices.reshape(8, 4, 4, 2), ALL)
    placed = (P(ALL, None), P(ALL, None), P(FSDP, None), P(ALL, None), P())
    return jax.shard_map(
        shards,
        mesh=split,
        in_specs=placed,
        out_specs=(P(ALL, None), P(ALL, None), P()),
        check_vma=False,
    )
```

```python
import functools

import jax
import jax.numpy as jnp
from jax import lax
from jax.experimental import pallas as pl
from jax.experimental.pallas import tpu as pltpu
from jax.sharding import Mesh, PartitionSpec as P

FSDP = ("y", "core")
ALL = ("z", "x", "y", "core")
BF16 = jnp.bfloat16
F32 = jnp.float32
VMEM = pl.BlockSpec(memory_space=pltpu.VMEM)
ANY = pl.BlockSpec(memory_space=pl.ANY)
SMEM = pl.BlockSpec(memory_space=pltpu.SMEM)
AHEAD = [(2 * y + c, 2 * ((y + 1 - 2 * c) % 4) + c) for y in range(4) for c in range(2)]
BACK = [(b, a) for a, b in AHEAD]
ACROSS = [(2 * y + c, 2 * ((y + 2) % 4) + c) for y in range(4) for c in range(2)]
HALF_Z, HALF_XY = (8, 6, 8, 128), (16, 3, 8, 128)


def mm(a, b, ca, cb):
    return lax.dot_general(a, b, (((ca,), (cb,)), ((), ())), preferred_element_type=F32)


def terms(v):
    a = v.astype(BF16)
    rest = v - a.astype(F32)
    b = rest.astype(BF16)
    return a, b, (rest - b.astype(F32)).astype(BF16)


def stacked(v):
    return jnp.concatenate(terms(v), axis=0)


def folded(v):
    return v[0:32] + v[32:64] + v[64:96]


def two_terms(v):
    return jnp.concatenate(terms(v)[:2], axis=0)


def put_window(place, feedback_ref, window_ref):
    core = place[0]
    zero = jnp.zeros((64, 2560), BF16)
    free = pl.multiple_of(320 * (1 - core), 64)
    first = pl.multiple_of(64 * core, 64)
    for i in range(5):
        rows = pl.ds(64 * i, 64)
        for t, term in enumerate(terms(feedback_ref[rows, :])[:2]):
            window_ref[t, pl.ds(pl.multiple_of(first + 64 * i, 64), 64), :] = term
    for t in range(2):
        window_ref[t, pl.ds(free, 64), :] = zero


class Copies:
    def __init__(self, sems):
        self.sems, self.made = sems, []

    def start(self, source, target):
        copy = pltpu.make_async_copy(source, target, self.sems.at[len(self.made)])
        copy.start()
        self.made.append(copy)
        return copy


def wait(copies):
    for copy in copies:
        copy.wait()


def emit(core, value, mine_ref, other_ref):
    for tile in range(48):
        if tile < 40:
            r, j = divmod(tile, 20)
            low = value[8 * r : 8 * r + 8, 128 * j : 128 * j + 128]
            high = value[16 + 8 * r : 24 + 8 * r, 128 * j : 128 * j + 128]
            mine, other = jnp.where(core == 0, low, high), jnp.where(core == 0, high, low)
        else:
            mine = other = jnp.zeros((8, 128), F32)
        at = divmod(tile, mine_ref.shape[1])
        mine_ref[at] = mine
        other_ref[at] = other


def collect(core, mine_ref, other_ref, whole_ref):
    for tile in range(40):
        r, j = divmod(tile, 20)
        at = divmod(tile, mine_ref.shape[1])
        mine, other = mine_ref[at], other_ref[at]
        lanes = pl.ds(128 * j, 128)
        whole_ref[pl.ds(8 * r, 8), lanes] = jnp.where(core == 0, mine, other)
        whole_ref[pl.ds(16 + 8 * r, 8), lanes] = jnp.where(core == 0, other, mine)


def left_kernel(
    place, x_any, c_any, s_ref, f_any, mine_ref, other_ref, sum_ref, x_ref, f_ref, c_ref, sems
):
    core, lane = place[0], pl.multiple_of(place[1], 128)
    copies = Copies(sems)

    def fetch(source, target, parts, rows):
        return [copies.start(source.at[pl.ds(rows * k, rows)], target.at[pl.ds(rows * k, rows)]) for k in parts]

    c_in = fetch(c_any, c_ref, range(4), 64)
    f_in = fetch(f_any, f_ref, range(10), 32)
    x_in = fetch(x_any, x_ref, range(4), 64)
    factors = jnp.concatenate(terms(s_ref[...].T), axis=1)
    wait(c_in)
    small = folded(mm(c_ref[...], factors, 1, 0).T)
    parts = []
    for k in range(2):
        wait(f_in[5 * k : 5 * k + 5])
        part = mm(two_terms(f_ref[pl.ds(160 * k, 160), :]), factors, 1, 0)
        parts.append(part[:160] + part[160:])
    own = folded(jnp.concatenate(parts, axis=0).T)
    zero = jnp.zeros((32, 64), F32)
    own = jnp.where(
        core == 0, jnp.concatenate([own, zero], axis=1), jnp.concatenate([zero, own], axis=1)
    )
    wait(x_in)
    sum_ref[...] = folded(mm(stacked(small), x_ref[...], 1, 0))
    sum_ref[:, pl.ds(lane, 384)] += own
    emit(core, sum_ref[...], mine_ref, other_ref)


def right_kernel(
    place, mine_ref, other_ref, x_any, c_any, f_any, out_ref, away_ref, gram_ref, own_ref,
    window_ref, left_ref, x_ref, c_ref, f_ref, sems,
):
    core, lane = place[0], pl.multiple_of(place[1], 128)
    copies = Copies(sems)
    x_in, f_in, c_in = copies.start(x_any, x_ref), copies.start(f_any, f_ref), copies.start(c_any, c_ref)
    collect(core, mine_ref, other_ref, left_ref)
    left = left_ref[...]
    own = left_ref[:, pl.ds(lane, 384)]
    own_ref[...] = own
    own3, p3 = stacked(own), stacked(left)
    gram_ref[...] = sum(folded(mm(p3, p3[32 * t : 32 * t + 32], 1, 1)) for t in range(3))
    x_in.wait()
    small = stacked(folded(mm(p3, x_ref[...], 1, 1)))
    f_in.wait()
    put_window(place, f_ref, window_ref)
    total = sum(mm(own3, window_ref[t], 1, 0) for t in range(2))
    c_in.wait()
    emit(core, folded(total + mm(small, c_ref[...], 1, 0)), out_ref, away_ref)


def back_kernel(place, c_ref, w_ref, out_ref):
    del place
    out_ref[...] = mm(c_ref[...], w_ref[...], 1, 1).astype(BF16)


def back_columns(place, c, weights):
    return pl.pallas_call(
        back_kernel,
        in_specs=[SMEM, VMEM, VMEM],
        out_specs=VMEM,
        out_shape=jax.ShapeDtypeStruct((256, 640), BF16),
        compiler_params=pltpu.CompilerParams(vmem_limit_bytes=16 << 20),
        cost_estimate=pl.CostEstimate(flops=84 * 10**7, bytes_accessed=5 << 20, transcendentals=0),
    )(place, c, weights)


def rows_kernel(place, *refs):
    xs, cs, f_any, mine_any, away_any = refs[:4], refs[4:8], refs[8], refs[9], refs[10]
    x_ref, turned, c_ref, f_ref, out_ref, sems = refs[11:]
    core, copies, parts = place[0], Copies(sems), []
    x_in = [copies.start(x, x_ref.at[pl.ds(256 * k, 256)]) for k, x in enumerate(xs)]
    for j in range(4):
        lanes = pl.ds(640 * j, 640)
        parts.append([copies.start(c.at[:, lanes], c_ref.at[pl.ds(256 * k, 256), lanes]) for k, c in enumerate(cs)])
    f_in = copies.start(f_any, f_ref)
    wait(x_in)
    first, last = pl.multiple_of(320 * core, 64), pl.multiple_of(320 * (1 - core), 64)
    for k in range(4):
        block = x_ref[pl.ds(256 * k, 256), :].T
        turned[pl.ds(first, 320), pl.ds(256 * k, 256)] = block[:320]
        turned[pl.ds(last, 320), pl.ds(256 * k, 256)] = block[320:]
    sent = []
    for j in range(4):
        lanes = pl.ds(640 * j, 640)
        wait(parts[j])
        out_ref[1, :, lanes] = mm(turned[pl.ds(320, 320), :], c_ref[:, lanes], 1, 0)
        sent.append(copies.start(out_ref.at[1, :, lanes], away_any.at[:, lanes]))
        out_ref[0, :, lanes] = mm(turned[pl.ds(0, 320), :], c_ref[:, lanes], 1, 0)
    f_in.wait()
    for j in range(4):
        rows = pl.ds(80 * j, 80)
        out_ref[0, rows, :] += f_ref[rows, :]
        sent.append(copies.start(out_ref.at[0, rows], mine_any.at[rows]))
    wait(sent)


def gradient_rows(place, xs, cs, feedback):
    return pl.pallas_call(
        rows_kernel,
        in_specs=[SMEM] + [ANY] * 9,
        out_specs=[ANY] * 2,
        out_shape=[jax.ShapeDtypeStruct((320, 2560), F32)] * 2,
        scratch_shapes=[pltpu.VMEM((1024, 640), BF16), pltpu.VMEM((640, 1024), BF16),
                        pltpu.VMEM((1024, 2560), BF16), pltpu.VMEM((320, 2560), F32),
                        pltpu.VMEM((2, 320, 2560), F32), pltpu.SemaphoreType.DMA((29,))],
        compiler_params=pltpu.CompilerParams(vmem_limit_bytes=119 << 19),
        cost_estimate=pl.CostEstimate(flops=34 * 10**8, bytes_accessed=17 << 20, transcendentals=0),
    )(place, *xs, *cs, feedback)


def place_kernel(place, g0, g1, g2, g3, out_ref):
    for k, g in enumerate((g0, g1, g2, g3)):
        out_ref[:, pl.ds(pl.multiple_of(640 * place[2 + k], 128), 640)] = g[...]


def placed_columns(place, blocks):
    return pl.pallas_call(
        place_kernel,
        in_specs=[SMEM] + [VMEM] * 4,
        out_specs=VMEM,
        out_shape=jax.ShapeDtypeStruct((256, 2560), BF16),
        cost_estimate=pl.CostEstimate(flops=0, bytes_accessed=3 << 20, transcendentals=0),
    )(place, *blocks)


def last_kernel(
    place, mine_ref, other_ref, inverse_ref, ortho_ref, grown_ref, new_any, q_ref,
    right_ref, lhs_ref, rhs_ref, new_ref, sems,
):
    copies = Copies(sems)
    collect(place[0], mine_ref, other_ref, right_ref)
    i1, i2, i3 = terms(inverse_ref[...])
    r1, r2, r3 = terms(right_ref[...])
    q = sum(mm(a, b, 1, 0) for a, b in ((i1, r1), (i1, r2), (i2, r1), (i2, r2), (i1, r3), (i3, r1)))
    q = q / 32
    q_ref[...] = q
    q1, q2, q3 = terms(q)
    o1, o2, o3 = terms(ortho_ref[...].T)
    for k, (o, q) in enumerate(((o1, q1), (o1, q2), (o2, q1), (o2, q2), (o1, q3), (o3, q1))):
        lhs_ref[:, pl.ds(32 * k, 32)] = o
        rhs_ref[pl.ds(32 * k, 32), :] = q
    for k in range(5):
        rows = pl.ds(64 * k, 64)
        lhs = lhs_ref[pl.ds(pl.multiple_of(64 * place[0] + 64 * k, 64), 64), :]
        new_ref[rows, :] = grown_ref[rows, :] - mm(lhs, rhs_ref[...], 1, 0)
        copies.start(new_ref.at[rows], new_any.at[rows])
    wait(copies.made)


def call(kernel, ins, outs, scratch, flops, size, limit=48):
    return pl.pallas_call(
        kernel,
        in_specs=[SMEM] + ins,
        out_specs=[VMEM] * len(outs),
        out_shape=[jax.ShapeDtypeStruct(s, F32) for s in outs],
        scratch_shapes=scratch,
        compiler_params=pltpu.CompilerParams(vmem_limit_bytes=limit << 19),
        cost_estimate=pl.CostEstimate(flops=flops, bytes_accessed=size, transcendentals=0),
    )


def left_product(place, x, c, s, f):
    return call(
        left_kernel, [ANY, ANY, VMEM, ANY], [HALF_Z, HALF_Z],
        [pltpu.VMEM((32, 2560), F32), pltpu.VMEM((256, 2560), BF16),
         pltpu.VMEM((320, 2560), F32), pltpu.VMEM((256, 2560), BF16),
         pltpu.SemaphoreType.DMA((18,))],
        2 * 10**9, 7 << 20, 119,
    )(place, x, c, s, f)


def right_product(place, mine, other, x, c, f):
    return call(
        right_kernel, [VMEM] * 2 + [ANY] * 3, [HALF_XY, HALF_XY, (32, 32), (32, 384)],
        [pltpu.VMEM((2, 384, 2560), BF16), pltpu.VMEM((32, 2560), F32),
         pltpu.VMEM((256, 2560), BF16), pltpu.VMEM((256, 2560), BF16),
         pltpu.VMEM((320, 2560), F32), pltpu.SemaphoreType.DMA((3,))],
        2 * 10**9, 7 << 20, 119,
    )(place, mine, other, x, c, f)


def factor_kernel(gram_ref, own_ref, inverse_ref, ortho_ref):
    row = lax.broadcasted_iota(jnp.int32, (32, 128), 0)
    lane = lax.broadcasted_iota(jnp.int32, (32, 128), 1)
    a = jnp.concatenate([gram_ref[...], jnp.zeros((32, 96), F32)], axis=1)
    a = jnp.where(lane == row + 32, 1.0, a)
    for j in range(32):
        column = a[:, j : j + 1] * (1.0 / a[j : j + 1, j : j + 1])
        a = jnp.where(row > j, a - column * a[j : j + 1, :], a)
    pivots = jnp.sum(jnp.where(lane == row, a, 0.0), axis=1, keepdims=True)
    inverse = a[:, 32:64] / jnp.sqrt(pivots)
    inverse_ref[...] = inverse
    i1, i2, i3 = terms(inverse)
    o1, o2, o3 = terms(own_ref[...])
    pairs = ((i1, o1), (i1, o2), (i2, o1), (i2, o2), (i1, o3), (i3, o1))
    ortho_ref[...] = sum(mm(a, b, 1, 0) for a, b in pairs)


def factor(gram, own):
    return pl.pallas_call(
        factor_kernel,
        in_specs=[VMEM] * 2,
        out_specs=[VMEM] * 2,
        out_shape=[jax.ShapeDtypeStruct((32, 32), F32), jax.ShapeDtypeStruct((32, 384), F32)],
        cost_estimate=pl.CostEstimate(flops=10**7, bytes_accessed=1 << 20, transcendentals=32),
    )(gram, own)


def last_step(place, mine, other, inverse, ortho, grown):
    return pl.pallas_call(
        last_kernel,
        in_specs=[SMEM] + [VMEM] * 5,
        out_specs=[ANY, VMEM],
        out_shape=[jax.ShapeDtypeStruct((320, 2560), F32), jax.ShapeDtypeStruct((32, 2560), F32)],
        scratch_shapes=[pltpu.VMEM((32, 2560), F32), pltpu.VMEM((384, 192), BF16),
                        pltpu.VMEM((192, 2560), BF16), pltpu.VMEM((320, 2560), F32),
                        pltpu.SemaphoreType.DMA((5,))],
        compiler_params=pltpu.CompilerParams(vmem_limit_bytes=24 << 20),
        cost_estimate=pl.CostEstimate(flops=3 * 10**8, bytes_accessed=8 << 20, transcendentals=0),
    )(place, mine, other, inverse, ortho, grown)


def exchange(u, axes):
    return lax.all_to_all(u, axes, 0, 0, tiled=True)


def swap(v):
    return lax.ppermute(v, "core", [(0, 1), (1, 0)])


def send(v, pairs):
    return lax.ppermute(v, FSDP, pairs)


def tie(*values):
    return lax.optimization_barrier(values)


def repeated(v, n):
    return jnp.broadcast_to(v.sum(0)[None], (n, *v.shape[1:]))


def shards(features, cotangent, weight, feedback, start_factors):
    core, y = lax.axis_index("core"), lax.axis_index("y")
    ahead, back = lax.rem(y + 5 - 2 * core, 4), lax.rem(y + 3 + 2 * core, 4)
    across = lax.rem(y + 2, 4)
    place = jnp.stack([core, 128 * (5 * y + 2 * core), y, ahead, back, across]).astype(jnp.int32)

    def columns(chip, x):
        return lax.dynamic_slice(x, (0, 640 * chip), (256, 640))

    c1, c2 = send(cotangent, AHEAD), send(cotangent, BACK)
    swapped = swap(weight)
    mine, other = left_product(place, features, cotangent, start_factors.T, feedback)

    half, later = tie(mine + swap(other), features)
    half = exchange(half, "z")
    x0, x1, x2, x3 = (columns(chip, later) for chip in (y, ahead, back, across))
    weights = jnp.where(
        core == 0, jnp.concatenate([weight, swapped]), jnp.concatenate([swapped, weight])
    )
    g0 = back_columns(place, cotangent, weights)
    half, g0, x0, x1, x2, x3 = tie(half, g0, x0, x1, x2, x3)
    half, x1, x2, x3 = tie(repeated(half, 16), x1, x2, x3)
    half = exchange(half, ("x", "y"))
    x1, x2, x3 = send(x1, AHEAD), send(x2, BACK), send(x3, ACROSS)
    half, c1, c2 = tie(half, c1, c2)
    half, c1, now = tie(repeated(half, 8), c1, place)
    half = exchange(half, "z")
    c3 = send(c1, AHEAD)
    g1, g2 = back_columns(now, c1, weights), back_columns(now, c2, weights)
    half, g1, g2 = tie(half, g1, g2)

    mine, other, gram, own = right_product(place, half, swap(half), features, cotangent, feedback)
    half, gram, own, g1, g2 = tie(mine + swap(other), gram, own, g1, g2)
    half = exchange(half, ("x", "y"))
    u1, u2 = send(g1, BACK), send(g2, AHEAD)
    inverse, ortho = factor(gram, own)
    inverse, ortho, now = tie(inverse, ortho, place)
    g3 = back_columns(now, c3, weights)
    half, ortho, inverse, g3 = tie(half, ortho, inverse, g3)
    half, g3, now = tie(repeated(half, 8), g3, place)
    half = exchange(half, "z")
    u3 = send(g3, ACROSS)
    grown, away = gradient_rows(now, (x0, x1, x2, x3), (cotangent, c1, c2, c3), feedback)
    half, u1, u2, grown, away = tie(half, u1, u2, grown, away)
    half, grown, away = tie(repeated(half, 16), grown, away)
    half = exchange(half, ("x", "y"))
    grown, now = tie(grown + swap(away), place)
    input_grad = placed_columns(now, (g0, u1, u2, u3))
    half, grown, input_grad = tie(half, grown, input_grad)

    new_feedback, q_factor = last_step(place, half, swap(half), inverse, ortho, grown)
    return (input_grad, new_feedback, q_factor.T)


def solution(mesh):
    split = Mesh(mesh.devices.reshape(8, 4, 4, 2), ALL)
    placed = (P(ALL, None), P(ALL, None), P(FSDP, None), P(ALL, None), P())
    return jax.shard_map(
        shards,
        mesh=split,
        in_specs=placed,
        out_specs=(P(ALL, None), P(ALL, None), P()),
        check_vma=False,
    )
```

```python
import functools

import jax
import jax.numpy as jnp
from jax import lax
from jax.experimental import pallas as pl
from jax.experimental.pallas import tpu as pltpu
from jax.sharding import Mesh, PartitionSpec as P

FSDP = ("y", "core")
ALL = ("z", "x", "y", "core")
BF16 = jnp.bfloat16
F32 = jnp.float32
VMEM = pl.BlockSpec(memory_space=pltpu.VMEM)
ANY = pl.BlockSpec(memory_space=pl.ANY)
SMEM = pl.BlockSpec(memory_space=pltpu.SMEM)
AHEAD = [(2 * y + c, 2 * ((y + 1 - 2 * c) % 4) + c) for y in range(4) for c in range(2)]
BACK = [(b, a) for a, b in AHEAD]
ACROSS = [(2 * y + c, 2 * ((y + 2) % 4) + c) for y in range(4) for c in range(2)]
HALF_Z, HALF_XY = (8, 6, 8, 128), (16, 3, 8, 128)


def mm(a, b, ca, cb):
    return lax.dot_general(a, b, (((ca,), (cb,)), ((), ())), preferred_element_type=F32)


def terms(v):
    a = v.astype(BF16)
    rest = v - a.astype(F32)
    b = rest.astype(BF16)
    return a, b, (rest - b.astype(F32)).astype(BF16)


def stacked(v):
    return jnp.concatenate(terms(v), axis=0)


def folded(v):
    return v[0:32] + v[32:64] + v[64:96]


def two_terms(v):
    return jnp.concatenate(terms(v)[:2], axis=0)


def put_window(place, feedback_ref, window_ref):
    core = place[0]
    zero = jnp.zeros((64, 2560), BF16)
    free = pl.multiple_of(320 * (1 - core), 64)
    first = pl.multiple_of(64 * core, 64)
    for i in range(5):
        rows = pl.ds(64 * i, 64)
        for t, term in enumerate(terms(feedback_ref[rows, :])[:2]):
            window_ref[t, pl.ds(pl.multiple_of(first + 64 * i, 64), 64), :] = term
    for t in range(2):
        window_ref[t, pl.ds(free, 64), :] = zero


class Copies:
    def __init__(self, sems):
        self.sems, self.made = sems, []

    def start(self, source, target):
        copy = pltpu.make_async_copy(source, target, self.sems.at[len(self.made)])
        copy.start()
        self.made.append(copy)
        return copy


def wait(copies):
    for copy in copies:
        copy.wait()


def emit(core, value, mine_ref, other_ref):
    for tile in range(48):
        if tile < 40:
            r, j = divmod(tile, 20)
            low = value[8 * r : 8 * r + 8, 128 * j : 128 * j + 128]
            high = value[16 + 8 * r : 24 + 8 * r, 128 * j : 128 * j + 128]
            mine, other = jnp.where(core == 0, low, high), jnp.where(core == 0, high, low)
        else:
            mine = other = jnp.zeros((8, 128), F32)
        at = divmod(tile, mine_ref.shape[1])
        mine_ref[at] = mine
        other_ref[at] = other


def collect(core, mine_ref, other_ref, whole_ref):
    for tile in range(40):
        r, j = divmod(tile, 20)
        at = divmod(tile, mine_ref.shape[1])
        mine, other = mine_ref[at], other_ref[at]
        lanes = pl.ds(128 * j, 128)
        whole_ref[pl.ds(8 * r, 8), lanes] = jnp.where(core == 0, mine, other)
        whole_ref[pl.ds(16 + 8 * r, 8), lanes] = jnp.where(core == 0, other, mine)


def left_kernel(
    x_any, c_any, s_ref, f_any, mine_ref, other_ref, sum_ref, x_ref, f_ref, c_ref, sems
):
    core = lax.axis_index("core")
    lane = pl.multiple_of(128 * (5 * lax.axis_index("y") + 2 * core), 128)
    copies = Copies(sems)

    def fetch(source, target, parts, rows):
        return [copies.start(source.at[pl.ds(rows * k, rows)], target.at[pl.ds(rows * k, rows)]) for k in parts]

    c_in = fetch(c_any, c_ref, range(4), 64)
    f_in = fetch(f_any, f_ref, range(10), 32)
    x_in = fetch(x_any, x_ref, range(4), 64)
    factors = jnp.concatenate(terms(s_ref[...].T), axis=1)
    wait(c_in)
    small = folded(mm(c_ref[...], factors, 1, 0).T)
    parts = []
    for k in range(2):
        wait(f_in[5 * k : 5 * k + 5])
        part = mm(two_terms(f_ref[pl.ds(160 * k, 160), :]), factors, 1, 0)
        parts.append(part[:160] + part[160:])
    own = folded(jnp.concatenate(parts, axis=0).T)
    zero = jnp.zeros((32, 64), F32)
    own = jnp.where(
        core == 0, jnp.concatenate([own, zero], axis=1), jnp.concatenate([zero, own], axis=1)
    )
    wait(x_in)
    sum_ref[...] = folded(mm(stacked(small), x_ref[...], 1, 0))
    sum_ref[:, pl.ds(lane, 384)] += own
    emit(core, sum_ref[...], mine_ref, other_ref)


def right_kernel(
    place, mine_ref, other_ref, x_any, c_any, f_any, out_ref, away_ref, gram_ref, own_ref,
    window_ref, left_ref, x_ref, c_ref, f_ref, sems,
):
    core, lane = place[0], pl.multiple_of(place[1], 128)
    copies = Copies(sems)
    x_in, f_in, c_in = copies.start(x_any, x_ref), copies.start(f_any, f_ref), copies.start(c_any, c_ref)
    collect(core, mine_ref, other_ref, left_ref)
    left = left_ref[...]
    own = left_ref[:, pl.ds(lane, 384)]
    own_ref[...] = own
    own3, p3 = stacked(own), stacked(left)
    gram_ref[...] = sum(folded(mm(p3, p3[32 * t : 32 * t + 32], 1, 1)) for t in range(3))
    x_in.wait()
    small = stacked(folded(mm(p3, x_ref[...], 1, 1)))
    f_in.wait()
    put_window(place, f_ref, window_ref)
    total = sum(mm(own3, window_ref[t], 1, 0) for t in range(2))
    c_in.wait()
    emit(core, folded(total + mm(small, c_ref[...], 1, 0)), out_ref, away_ref)


def back_kernel(place, c_ref, w_ref, out_ref):
    del place
    out_ref[...] = mm(c_ref[...], w_ref[...], 1, 1).astype(BF16)


def back_columns(place, c, weights):
    return pl.pallas_call(
        back_kernel,
        in_specs=[SMEM, VMEM, VMEM],
        out_specs=VMEM,
        out_shape=jax.ShapeDtypeStruct((256, 640), BF16),
        compiler_params=pltpu.CompilerParams(vmem_limit_bytes=16 << 20),
        cost_estimate=pl.CostEstimate(flops=84 * 10**7, bytes_accessed=5 << 20, transcendentals=0),
    )(place, c, weights)


def rows_kernel(place, *refs):
    xs, cs, f_any, mine_any, away_any = refs[:4], refs[4:8], refs[8], refs[9], refs[10]
    x_ref, turned, c_ref, f_ref, out_ref, sems = refs[11:]
    core, copies, parts = place[0], Copies(sems), []
    x_in = [copies.start(x, x_ref.at[pl.ds(256 * k, 256)]) for k, x in enumerate(xs)]
    for j in range(4):
        lanes = pl.ds(640 * j, 640)
        parts.append([copies.start(c.at[:, lanes], c_ref.at[pl.ds(256 * k, 256), lanes]) for k, c in enumerate(cs)])
    f_in = copies.start(f_any, f_ref)
    wait(x_in)
    first, last = pl.multiple_of(320 * core, 64), pl.multiple_of(320 * (1 - core), 64)
    for k in range(4):
        block = x_ref[pl.ds(256 * k, 256), :].T
        turned[pl.ds(first, 320), pl.ds(256 * k, 256)] = block[:320]
        turned[pl.ds(last, 320), pl.ds(256 * k, 256)] = block[320:]
    sent = []
    for j in range(4):
        lanes = pl.ds(640 * j, 640)
        wait(parts[j])
        out_ref[1, :, lanes] = mm(turned[pl.ds(320, 320), :], c_ref[:, lanes], 1, 0)
        sent.append(copies.start(out_ref.at[1, :, lanes], away_any.at[:, lanes]))
        out_ref[0, :, lanes] = mm(turned[pl.ds(0, 320), :], c_ref[:, lanes], 1, 0)
    f_in.wait()
    for j in range(4):
        rows = pl.ds(80 * j, 80)
        out_ref[0, rows, :] += f_ref[rows, :]
        sent.append(copies.start(out_ref.at[0, rows], mine_any.at[rows]))
    wait(sent)


def gradient_rows(place, xs, cs, feedback):
    return pl.pallas_call(
        rows_kernel,
        in_specs=[SMEM] + [ANY] * 9,
        out_specs=[ANY] * 2,
        out_shape=[jax.ShapeDtypeStruct((320, 2560), F32)] * 2,
        scratch_shapes=[pltpu.VMEM((1024, 640), BF16), pltpu.VMEM((640, 1024), BF16),
                        pltpu.VMEM((1024, 2560), BF16), pltpu.VMEM((320, 2560), F32),
                        pltpu.VMEM((2, 320, 2560), F32), pltpu.SemaphoreType.DMA((29,))],
        compiler_params=pltpu.CompilerParams(vmem_limit_bytes=119 << 19),
        cost_estimate=pl.CostEstimate(flops=34 * 10**8, bytes_accessed=17 << 20, transcendentals=0),
    )(place, *xs, *cs, feedback)


def place_kernel(place, g0, g1, g2, g3, out_ref):
    for k, g in enumerate((g0, g1, g2, g3)):
        out_ref[:, pl.ds(pl.multiple_of(640 * place[2 + k], 128), 640)] = g[...]


def placed_columns(place, blocks):
    return pl.pallas_call(
        place_kernel,
        in_specs=[SMEM] + [VMEM] * 4,
        out_specs=VMEM,
        out_shape=jax.ShapeDtypeStruct((256, 2560), BF16),
        cost_estimate=pl.CostEstimate(flops=0, bytes_accessed=3 << 20, transcendentals=0),
    )(place, *blocks)


def last_kernel(
    place, mine_ref, other_ref, inverse_ref, ortho_ref, grown_ref, new_any, q_ref,
    right_ref, lhs_ref, rhs_ref, new_ref, sems,
):
    copies = Copies(sems)
    collect(place[0], mine_ref, other_ref, right_ref)
    i1, i2, i3 = terms(inverse_ref[...])
    r1, r2, r3 = terms(right_ref[...])
    q = sum(mm(a, b, 1, 0) for a, b in ((i1, r1), (i1, r2), (i2, r1), (i2, r2), (i1, r3), (i3, r1)))
    q = q / 32
    q_ref[...] = q
    q1, q2, q3 = terms(q)
    o1, o2, o3 = terms(ortho_ref[...].T)
    for k, (o, q) in enumerate(((o1, q1), (o1, q2), (o2, q1), (o2, q2), (o1, q3), (o3, q1))):
        lhs_ref[:, pl.ds(32 * k, 32)] = o
        rhs_ref[pl.ds(32 * k, 32), :] = q
    for k in range(5):
        rows = pl.ds(64 * k, 64)
        lhs = lhs_ref[pl.ds(pl.multiple_of(64 * place[0] + 64 * k, 64), 64), :]
        new_ref[rows, :] = grown_ref[rows, :] - mm(lhs, rhs_ref[...], 1, 0)
        copies.start(new_ref.at[rows], new_any.at[rows])
    wait(copies.made)


def call(kernel, ins, outs, scratch, flops, size, limit=48):
    return pl.pallas_call(
        kernel,
        in_specs=ins,
        out_specs=[VMEM] * len(outs),
        out_shape=[jax.ShapeDtypeStruct(s, F32) for s in outs],
        scratch_shapes=scratch,
        compiler_params=pltpu.CompilerParams(vmem_limit_bytes=limit << 19),
        cost_estimate=pl.CostEstimate(flops=flops, bytes_accessed=size, transcendentals=0),
    )


def left_product(x, c, s, f):
    return call(
        left_kernel, [ANY, ANY, VMEM, ANY], [HALF_Z, HALF_Z],
        [pltpu.VMEM((32, 2560), F32), pltpu.VMEM((256, 2560), BF16),
         pltpu.VMEM((320, 2560), F32), pltpu.VMEM((256, 2560), BF16),
         pltpu.SemaphoreType.DMA((18,))],
        2 * 10**9, 7 << 20, 119,
    )(x, c, s, f)


def right_product(place, mine, other, x, c, f):
    return call(
        right_kernel, [SMEM] + [VMEM] * 2 + [ANY] * 3, [HALF_XY, HALF_XY, (32, 32), (32, 384)],
        [pltpu.VMEM((2, 384, 2560), BF16), pltpu.VMEM((32, 2560), F32),
         pltpu.VMEM((256, 2560), BF16), pltpu.VMEM((256, 2560), BF16),
         pltpu.VMEM((320, 2560), F32), pltpu.SemaphoreType.DMA((3,))],
        2 * 10**9, 7 << 20, 119,
    )(place, mine, other, x, c, f)


def factor_kernel(gram_ref, own_ref, inverse_ref, ortho_ref):
    row = lax.broadcasted_iota(jnp.int32, (32, 128), 0)
    lane = lax.broadcasted_iota(jnp.int32, (32, 128), 1)
    a = jnp.concatenate([gram_ref[...], jnp.zeros((32, 96), F32)], axis=1)
    a = jnp.where(lane == row + 32, 1.0, a)
    for j in range(32):
        column = a[:, j : j + 1] * (1.0 / a[j : j + 1, j : j + 1])
        a = jnp.where(row > j, a - column * a[j : j + 1, :], a)
    pivots = jnp.sum(jnp.where(lane == row, a, 0.0), axis=1, keepdims=True)
    inverse = a[:, 32:64] / jnp.sqrt(pivots)
    inverse_ref[...] = inverse
    i1, i2, i3 = terms(inverse)
    o1, o2, o3 = terms(own_ref[...])
    pairs = ((i1, o1), (i1, o2), (i2, o1), (i2, o2), (i1, o3), (i3, o1))
    ortho_ref[...] = sum(mm(a, b, 1, 0) for a, b in pairs)


def factor(gram, own):
    return pl.pallas_call(
        factor_kernel,
        in_specs=[VMEM] * 2,
        out_specs=[VMEM] * 2,
        out_shape=[jax.ShapeDtypeStruct((32, 32), F32), jax.ShapeDtypeStruct((32, 384), F32)],
        cost_estimate=pl.CostEstimate(flops=10**7, bytes_accessed=1 << 20, transcendentals=32),
    )(gram, own)


def last_step(place, mine, other, inverse, ortho, grown):
    return pl.pallas_call(
        last_kernel,
        in_specs=[SMEM] + [VMEM] * 5,
        out_specs=[ANY, VMEM],
        out_shape=[jax.ShapeDtypeStruct((320, 2560), F32), jax.ShapeDtypeStruct((32, 2560), F32)],
        scratch_shapes=[pltpu.VMEM((32, 2560), F32), pltpu.VMEM((384, 192), BF16),
                        pltpu.VMEM((192, 2560), BF16), pltpu.VMEM((320, 2560), F32),
                        pltpu.SemaphoreType.DMA((5,))],
        compiler_params=pltpu.CompilerParams(vmem_limit_bytes=24 << 20),
        cost_estimate=pl.CostEstimate(flops=3 * 10**8, bytes_accessed=8 << 20, transcendentals=0),
    )(place, mine, other, inverse, ortho, grown)


def exchange(u, axes):
    return lax.all_to_all(u, axes, 0, 0, tiled=True)


def swap(v):
    return lax.ppermute(v, "core", [(0, 1), (1, 0)])


def send(v, pairs):
    return lax.ppermute(v, FSDP, pairs)


def tie(*values):
    return lax.optimization_barrier(values)


def repeated(v, n):
    return jnp.broadcast_to(v.sum(0)[None], (n, *v.shape[1:]))


def shards(features, cotangent, weight, feedback, start_factors):
    core, y = lax.axis_index("core"), lax.axis_index("y")
    ahead, back = lax.rem(y + 5 - 2 * core, 4), lax.rem(y + 3 + 2 * core, 4)
    across = lax.rem(y + 2, 4)
    place = jnp.stack([core, 128 * (5 * y + 2 * core), y, ahead, back, across]).astype(jnp.int32)

    def columns(chip, x):
        return lax.dynamic_slice(x, (0, 640 * chip), (256, 640))

    c1, c2 = send(cotangent, AHEAD), send(cotangent, BACK)
    swapped = swap(weight)
    mine, other = left_product(features, cotangent, start_factors.T, feedback)

    half, later = tie(mine + swap(other), features)
    half = exchange(half, "z")
    x0, x1, x2, x3 = (columns(chip, later) for chip in (y, ahead, back, across))
    weights = jnp.where(
        core == 0, jnp.concatenate([weight, swapped]), jnp.concatenate([swapped, weight])
    )
    g0 = back_columns(place, cotangent, weights)
    half, g0, x0, x1, x2, x3 = tie(half, g0, x0, x1, x2, x3)
    half, x1, x2, x3 = tie(repeated(half, 16), x1, x2, x3)
    half = exchange(half, ("x", "y"))
    x1, x2, x3 = send(x1, AHEAD), send(x2, BACK), send(x3, ACROSS)
    half, c1, c2 = tie(half, c1, c2)
    half, c1, now = tie(repeated(half, 8), c1, place)
    half = exchange(half, "z")
    c3 = send(c1, AHEAD)
    g1, g2 = back_columns(now, c1, weights), back_columns(now, c2, weights)
    half, g1, g2 = tie(half, g1, g2)

    mine, other, gram, own = right_product(place, half, swap(half), features, cotangent, feedback)
    half, gram, own, g1, g2 = tie(mine + swap(other), gram, own, g1, g2)
    half = exchange(half, ("x", "y"))
    u1, u2 = send(g1, BACK), send(g2, AHEAD)
    inverse, ortho = factor(gram, own)
    inverse, ortho, now = tie(inverse, ortho, place)
    g3 = back_columns(now, c3, weights)
    half, ortho, inverse, g3 = tie(half, ortho, inverse, g3)
    half, g3, now = tie(repeated(half, 8), g3, place)
    half = exchange(half, "z")
    u3 = send(g3, ACROSS)
    grown, away = gradient_rows(now, (x0, x1, x2, x3), (cotangent, c1, c2, c3), feedback)
    half, u1, u2, grown, away = tie(half, u1, u2, grown, away)
    half, grown, away = tie(repeated(half, 16), grown, away)
    half = exchange(half, ("x", "y"))
    grown, now = tie(grown + swap(away), place)
    input_grad = placed_columns(now, (g0, u1, u2, u3))
    half, grown, input_grad = tie(half, grown, input_grad)

    new_feedback, q_factor = last_step(place, half, swap(half), inverse, ortho, grown)
    return (input_grad, new_feedback, q_factor.T)


def solution(mesh):
    split = Mesh(mesh.devices.reshape(8, 4, 4, 2), ALL)
    placed = (P(ALL, None), P(ALL, None), P(FSDP, None), P(ALL, None), P())
    return jax.shard_map(
        shards,
        mesh=split,
        in_specs=placed,
        out_specs=(P(ALL, None), P(ALL, None), P()),
        check_vma=False,
    )
```
